32 devices in a mesh: row: 8 (over y, x, core), col: 4 (over z).
Axes of the slice: x: 2, y: 2, z: 4, core: 2. Of those that a mesh axis runs over, the one named last changes fastest.
Arguments:
- inputs: bfloat16 [1024, 14848], P('col', 'row'), may hold values from -6 to 6
- cotangent: bfloat16 [1024, 30720], P('col', 'row'), may hold values from -0.29882812 to 0.29882812
- weight: bfloat16 [14848, 30720], P('col', 'row'), may hold values from -0.046875 to 0.046875
- adapter_down_factor: bfloat16 [14848, 16], replicated, may hold values from -0.046875 to 0.046875
- adapter_up_factor: bfloat16 [16, 30720], replicated, may hold values from -1.5 to 1.5
Outputs:
- grad_input: bfloat16 [1024, 14848], P('row', 'col')
- grad_a: float32 [14848, 16], P('row')
- grad_b: float32 [16, 30720], P(None, 'row')
The draws below stay inside these ranges and needn't reach their ends.
All inputs are finite; a program needn't handle non-finite values.
Results may differ from the reference program's by a relative error of at most 0.001.
Values may be sent and summed in bfloat16 or wider, within the bound.
A program may use at most 128 MiB of HBM per device.

```python
import jax
import jax.numpy as jnp
from jax import lax

MODEL_WIDTH = 14848
HIDDEN_UNITS = 30720
ADAPTER_RANK = 16
TOK = 1024


def block_scale(key, shape, shards, least, high):
    def one(position, parts):
        draws = jax.random.uniform(jax.random.fold_in(jax.random.fold_in(key, 6), position), (parts,), jnp.float32, least / len(shards), high / len(shards))
        return jnp.repeat(jnp.exp(draws), shape[position] // parts).reshape((-1,) + (1,) * (len(shape) - position - 1))

    loudness = one(*shards[0])
    for cut in shards[1:]:
        loudness = loudness * one(*cut)
    return loudness


def gaussian(stream_key, extent, deviation, reach, cuts=(), kind=jnp.bfloat16):
    result = jax.random.normal(stream_key, extent, jnp.float32) * deviation
    if len(cuts) > 0:
        result = block_scale(stream_key, extent, cuts, -0.22, 0.18) * result
    return jnp.clip(result, min=-reach, max=reach).astype(kind)


def setup_inputs(seed: int = 0) -> dict:
    streams_of = jax.random.split(jax.random.key(seed), 6)
    inputs = gaussian(streams_of[0], (TOK, MODEL_WIDTH), 1.0, 6.0, ((0, 4), (1, 8)))
    cotangent = gaussian(streams_of[1], (TOK, HIDDEN_UNITS), 0.05, 0.29882812, ((0, 4), (1, 8)))
    weight = gaussian(streams_of[2], (MODEL_WIDTH, HIDDEN_UNITS), MODEL_WIDTH ** -0.5, 0.046875, ((0, 4), (1, 8)))
    adapter_down_factor = gaussian(streams_of[3], (MODEL_WIDTH, ADAPTER_RANK), MODEL_WIDTH ** -0.5, 0.046875)
    adapter_up_factor = gaussian(streams_of[4], (ADAPTER_RANK, HIDDEN_UNITS), ADAPTER_RANK ** -0.5, 1.5)
    return {"inputs": inputs, "cotangent": cotangent, "weight": weight, "adapter_down_factor": adapter_down_factor, "adapter_up_factor": adapter_up_factor}


scaling = 2.0


def wide_product(left, right):
    return jnp.dot(left.astype(jnp.float32), right.astype(jnp.float32), precision=lax.Precision.HIGHEST)


def reference(inputs, cotangent, weight, adapter_down_factor, adapter_up_factor):
    base = wide_product(cotangent, weight.T)
    gradient_lowrank = wide_product(cotangent, adapter_up_factor.T)
    projected_rows = wide_product(inputs, adapter_down_factor)
    adapter_factor = adapter_down_factor.astype(jnp.float32)
    inputs_wide = inputs.astype(jnp.float32)
    grad_input = (base + scaling * jnp.dot(gradient_lowrank, adapter_factor.T, precision=lax.Precision.HIGHEST)).astype(jnp.bfloat16)
    grad_a = scaling * jnp.dot(inputs_wide.T, gradient_lowrank, precision=lax.Precision.HIGHEST)
    grad_b = scaling * jnp.dot(projected_rows.T, cotangent.astype(jnp.float32), precision=lax.Precision.HIGHEST)
    return grad_input, grad_a, grad_b
```

```python
import functools

import jax
import jax.numpy as jnp
from jax import lax
from jax.experimental import pallas as pl
from jax.experimental.pallas import tpu as pltpu
from jax.sharding import PartitionSpec as P

scaling = 2.0
MESH = pl.DeviceIdType.MESH
CHUNK = 64
SLOTS = 4


def contract_trailing_axis(left, right):
    return lax.dot_general(
        left, right, (((1,), (1,)), ((), ())), preferred_element_type=jnp.float32
    )


def input_gradient_kernel(
    n, rows, cot_hbm, weight_hbm, up3, down3, out,
    gathered, weight, part, core_in, half, arrive, fin,
    load_sem, zsend, zrecv, core_send, core_recv, quarter_send, arrive_sem,
    fin_send, fin_recv, credit,
):
    z = lax.axis_index("col")
    r = lax.axis_index("row")
    core = r % 2
    x = (r // 2) % 2
    y = r // 4
    ny = rows // 4
    shard = cot_hbm.shape[0]
    width = weight_hbm.shape[0]
    m = CHUNK
    chunks = shard // m
    total = n * chunks
    own_rows = out.shape[0]
    h2, h4 = m // 2, m // 4
    partner = {"row": r + 1 - 2 * core}
    x_peer = {"row": y * 4 + (1 - x) * 2 + core}

    def y_peer(step):
        return {"row": ((y + step) % ny) * 4 + x * 2 + core}

    load_weight = pltpu.make_async_copy(weight_hbm, weight, load_sem.at[0])
    load_own = pltpu.make_async_copy(
        cot_hbm, gathered.at[pl.ds(pl.multiple_of(z * shard, 16), shard)], load_sem.at[1]
    )
    load_own.start()
    load_weight.start()

    barrier = pltpu.get_barrier_semaphore()
    peers = [partner, x_peer] + [y_peer(k) for k in range(1, ny)]
    for peer in peers:
        pl.semaphore_signal(barrier, inc=1, device_id=peer, device_id_type=MESH)

    @pl.when(z > 0)
    def _():
        pl.semaphore_signal(barrier, inc=1, device_id={"col": z - 1}, device_id_type=MESH)

    @pl.when(z < n - 1)
    def _():
        pl.semaphore_signal(barrier, inc=1, device_id={"col": z + 1}, device_id_type=MESH)

    ends = jnp.where(z > 0, 1, 0) + jnp.where(z < n - 1, 1, 0)
    pl.semaphore_wait(barrier, len(peers) + ends)
    load_own.wait()

    def rows_of(s, c):
        return pl.ds(pl.multiple_of(s * shard + c * m, 16), m)

    def z_copy(s, c, side, target):
        block = gathered.at[rows_of(s, c)]
        return pltpu.make_async_remote_copy(
            src_ref=block,
            dst_ref=block,
            send_sem=zsend.at[side, s * chunks + c],
            recv_sem=zrecv.at[s * chunks + c],
            device_id={"col": target},
            device_id_type=MESH,
        )

    def pass_left(s, c):
        @pl.when(z > 0)
        def _():
            z_copy(s, c, 0, z - 1).start()

    def pass_right(s, c):
        @pl.when(z < n - 1)
        def _():
            z_copy(s, c, 1, z + 1).start()

    pass_left(z, 0)
    pass_right(z, 0)

    pairs = jnp.minimum(z, n - 1 - z)

    def place(i):
        c, p = i // n, i % n
        near = (p + 1) // 2
        near_shard = jnp.where(p % 2 == 1, z + near, z - near)
        far = p - pairs
        far_shard = jnp.where(z < n - 1 - z, z + far, z - far)
        s = jnp.where(p <= 2 * pairs, near_shard, far_shard)
        token = s * shard + c * m
        dest = token // own_rows
        return c, p, s, dest, token % own_rows

    def copy_core(slot):
        return pltpu.make_async_remote_copy(
            src_ref=part.at[pl.ds(pl.multiple_of((1 - core) * h2, 8), h2)],
            dst_ref=core_in.at[slot],
            send_sem=core_send.at[slot],
            recv_sem=core_recv.at[slot],
            device_id=partner,
            device_id_type=MESH,
        )

    def copy_quarter(slot, q, landing, target):
        return pltpu.make_async_remote_copy(
            src_ref=half.at[slot, pl.ds(q * h4, h4)],
            dst_ref=arrive.at[slot, landing],
            send_sem=quarter_send.at[slot, q],
            recv_sem=arrive_sem.at[slot, landing],
            device_id=target,
            device_id_type=MESH,
        )

    def first_hop(slot, dest):
        yd, xd = dest // 4, (dest // 2) % 2

        @pl.when(y != yd)
        def _():
            landing = 2 + (y - yd + ny) % ny - 1
            copy_quarter(slot, 0, landing, {"row": yd * 4 + x * 2 + core}).start()

        @pl.when(x != xd)
        def _():
            copy_quarter(slot, 1, 0, x_peer).start()

    def wait_landing(slot, landing):
        copy_quarter(slot, 0, landing, x_peer).wait_recv()

    def second_hop(i):
        _, _, _, dest, _ = place(i)
        slot = i % SLOTS
        yd, xd = dest // 4, (dest // 2) % 2

        @pl.when(y == yd)
        def _():
            for k in range(ny - 1):
                wait_landing(slot, 2 + k)
                half[slot, pl.ds(0, h4)] += arrive[slot, 2 + k]

            @pl.when(x != xd)
            def _():
                copy_quarter(slot, 0, 1, x_peer).start()

        @pl.when(x == xd)
        def _():
            wait_landing(slot, 0)
            half[slot, pl.ds(h4, h4)] += arrive[slot, 0]

            @pl.when(y != yd)
            def _():
                landing = 2 + ny - 1 + (y - yd + ny) % ny - 1
                copy_quarter(slot, 1, landing, {"row": yd * 4 + x * 2 + core}).start()

    def fin_copy(start, index):
        return pltpu.make_async_remote_copy(
            src_ref=fin,
            dst_ref=out.at[pl.ds(pl.multiple_of(start, 16), h2)],
            send_sem=fin_send.at[0],
            recv_sem=fin_recv.at[index],
            device_id=partner,
            device_id_type=MESH,
        )

    def finish(i):
        _, _, _, dest, local = place(i)
        slot = i % SLOTS
        yd, xd, cored = dest // 4, (dest // 2) % 2, dest % 2
        here = jnp.logical_and(y == yd, x == xd)

        @pl.when(here)
        def _():
            wait_landing(slot, 1)
            half[slot, pl.ds(0, h4)] += arrive[slot, 1]
            for k in range(ny - 1):
                wait_landing(slot, 2 + ny - 1 + k)
                half[slot, pl.ds(h4, h4)] += arrive[slot, 2 + ny - 1 + k]
            start = local + core * h2

            @pl.when(core == cored)
            def _():
                out[pl.ds(pl.multiple_of(start, 16), h2)] = half[slot].astype(jnp.bfloat16)

            @pl.when(core != cored)
            def _():
                fin[...] = half[slot].astype(jnp.bfloat16)
                copy = fin_copy(start, local // m)
                copy.start()
                copy.wait_send()

        @pl.when(jnp.logical_not(here))
        def _():
            copy_quarter(slot, 0, 0, x_peer).wait_send()
            copy_quarter(slot, 1, 0, x_peer).wait_send()

        @pl.when(i < total - SLOTS)
        def _():
            for k, peer in enumerate(peers):
                index = k if k < 2 else 2 + (ny - (k - 1)) - 1
                pl.semaphore_signal(credit.at[index], inc=1, device_id=peer, device_id_type=MESH)

    block = min(256, width)
    whole_blocks = width // block

    def multiply(block_rows, low):
        def columns(start, size):
            value = contract_trailing_axis(block_rows, weight[pl.ds(start, size)])
            part[:, pl.ds(start, size)] = value + contract_trailing_axis(
                low, down3[pl.ds(start, size)]
            )

        @pl.loop(0, whole_blocks)
        def _(j):
            columns(pl.multiple_of(j * block, block), block)

        if width % block:
            columns(whole_blocks * block, width % block)

    @pl.loop(0, total)
    def _(i):
        c, p, s, dest, _ = place(i)
        slot = i % SLOTS

        @pl.when(jnp.logical_and(p == 0, c + 1 < chunks))
        def _():
            pass_left(z, c + 1)
            pass_right(z, c + 1)

        @pl.when(s != z)
        def _():
            z_copy(s, c, 0, z).wait_recv()

        @pl.when(s > z)
        def _():
            pass_left(s, c)

        @pl.when(s < z)
        def _():
            pass_right(s, c)

        @pl.when(i == 0)
        def _():
            load_weight.wait()

        block_rows = gathered[rows_of(s, c)]
        rank3 = up3.shape[0]
        rank = rank3 // 3
        low = contract_trailing_axis(block_rows, up3[...])
        high = low.astype(jnp.bfloat16)
        rest = low - high.astype(jnp.float32)
        middle = rest.astype(jnp.bfloat16)
        last = (rest - middle.astype(jnp.float32)).astype(jnp.bfloat16)
        lane = lax.broadcasted_iota(jnp.int32, low.shape, 1)
        split = jnp.where(
            lane < rank,
            high.astype(jnp.float32),
            jnp.where(lane < 2 * rank, middle.astype(jnp.float32), last.astype(jnp.float32)),
        ).astype(jnp.bfloat16)
        multiply(block_rows, split)

        @pl.when(i >= SLOTS)
        def _():
            for k in range(len(peers)):
                pl.semaphore_wait(credit.at[k], 1)

        exchange = copy_core(slot)
        exchange.start()
        exchange.wait()
        half[slot] = part[pl.ds(pl.multiple_of(core * h2, 8), h2)] + core_in[slot]
        first_hop(slot, dest)

        @pl.when(i >= 1)
        def _():
            second_hop(i - 1)

        @pl.when(i >= 2)
        def _():
            finish(i - 2)

    second_hop(total - 1)
    finish(total - 2)
    finish(total - 1)

    for index in range(own_rows // m):
        fin_copy(index * m, index).wait_recv()

    @pl.loop(0, total)
    def _(i):
        c, _, s, _, _ = place(i)

        @pl.when(jnp.logical_and(z > 0, s >= z))
        def _():
            z_copy(s, c, 0, z).wait_send()

        @pl.when(jnp.logical_and(z < n - 1, s <= z))
        def _():
            z_copy(s, c, 1, z).wait_send()


def input_gradient(n, rows, cotangent, weight, up_slice, down_slice):
    shard, hidden = cotangent.shape
    width = weight.shape[0]
    tokens = shard * n
    m = CHUNK
    total = tokens // m
    ny = rows // 4
    own_rows = tokens // rows
    up3 = jnp.concatenate([up_slice] * 3, axis=0)
    down3 = jnp.concatenate([down_slice * jnp.bfloat16(scaling)] * 3, axis=1)
    vmem = pl.BlockSpec(memory_space=pltpu.VMEM)
    hbm = pl.BlockSpec(memory_space=pl.ANY)
    return pl.pallas_call(
        functools.partial(input_gradient_kernel, n, rows),
        out_shape=jax.ShapeDtypeStruct((own_rows, width), jnp.bfloat16),
        in_specs=[hbm, hbm, vmem, vmem],
        out_specs=vmem,
        scratch_shapes=[
            pltpu.VMEM((tokens, hidden), jnp.bfloat16),
            pltpu.VMEM((width, hidden), jnp.bfloat16),
            pltpu.VMEM((m, width), jnp.float32),
            pltpu.VMEM((SLOTS, m // 2, width), jnp.float32),
            pltpu.VMEM((SLOTS, m // 2, width), jnp.float32),
            pltpu.VMEM((SLOTS, 2 * ny, m // 4, width), jnp.float32),
            pltpu.VMEM((m // 2, width), jnp.bfloat16),
            pltpu.SemaphoreType.DMA((2,)),
            pltpu.SemaphoreType.DMA((2, total)),
            pltpu.SemaphoreType.DMA((total,)),
            pltpu.SemaphoreType.DMA((SLOTS,)),
            pltpu.SemaphoreType.DMA((SLOTS,)),
            pltpu.SemaphoreType.DMA((SLOTS, 2)),
            pltpu.SemaphoreType.DMA((SLOTS, 2 * ny)),
            pltpu.SemaphoreType.DMA((1,)),
            pltpu.SemaphoreType.DMA((own_rows // m,)),
            pltpu.SemaphoreType.REGULAR((ny + 1,)),
        ],
        compiler_params=pltpu.CompilerParams(
            collective_id=0, has_side_effects=True, vmem_limit_bytes=62 * 2**20
        ),
        cost_estimate=pl.CostEstimate(
            flops=2 * tokens * width * hidden,
            bytes_accessed=2 * width * hidden,
            transcendentals=0,
        ),
        name="input_gradient",
    )(cotangent, weight, up3, down3)


def on_device(n, rows, inputs, cotangent, weight, adapter_down_factor, adapter_up_factor):
    row_position = lax.axis_index("row")
    column_position = lax.axis_index("col")
    width_row_block = inputs.shape[1]
    width_columns = weight.shape[0]
    hidden_columns = cotangent.shape[1]
    down_factor_rows = lax.dynamic_slice_in_dim(
        adapter_down_factor, row_position * width_row_block, width_row_block, 0
    )
    down_factor_columns = lax.dynamic_slice_in_dim(
        adapter_down_factor, column_position * width_columns, width_columns, 0
    )
    up_weight_slice = lax.dynamic_slice_in_dim(
        adapter_up_factor, row_position * hidden_columns, hidden_columns, 1
    )
    grad_input = input_gradient(
        n, rows, cotangent, weight, up_weight_slice, down_factor_columns
    )
    low_part = contract_trailing_axis(cotangent, up_weight_slice)
    proj_part = jnp.dot(inputs, down_factor_rows, preferred_element_type=jnp.float32)
    gradient_lowrank, projected_rows = lax.psum((low_part, proj_part), "row")
    part_a = scaling * jnp.dot(
        inputs.astype(jnp.float32).T, gradient_lowrank, precision=lax.Precision.HIGHEST
    )
    part_b = scaling * jnp.dot(
        projected_rows.T, cotangent.astype(jnp.float32), precision=lax.Precision.HIGHEST
    )
    grad_a, grad_b = lax.psum((part_a, part_b), "col")
    return (grad_input, grad_a, grad_b)


def solution(mesh):
    in_specs = (P("col", "row"), P("col", "row"), P("col", "row"), P(), P())
    out_specs = (P("row", "col"), P("row", None), P(None, "row"))
    body = functools.partial(on_device, mesh.shape["col"], mesh.shape["row"])
    return jax.shard_map(
        body, mesh=mesh, in_specs=in_specs, out_specs=out_specs, check_vma=False
    )
```

```python
import functools

import jax
import jax.numpy as jnp
from jax import lax
from jax.experimental import pallas as pl
from jax.experimental.pallas import tpu as pltpu
from jax.sharding import PartitionSpec as P

scaling = 2.0
MESH = pl.DeviceIdType.MESH
CHUNK = 64


def contract_trailing_axis(left, right):
    return lax.dot_general(
        left, right, (((1,), (1,)), ((), ())), preferred_element_type=jnp.float32
    )


def input_gradient_kernel(
    n, rows, batches, cot_hbm, weight_hbm, up3, down3, out,
    gathered, weight, part, core_in, half, arrive, fin,
    load_sem, zsend, zrecv, core_send, core_recv, quarter_send, arrive_sem,
    fin_send, fin_recv, credit,
):
    z = lax.axis_index("col")
    r = lax.axis_index("row")
    core = r % 2
    x = (r // 2) % 2
    y = r // 4
    ny = rows // 4
    shard = cot_hbm.shape[0]
    width = weight_hbm.shape[0]
    m = CHUNK
    chunks = shard // m
    total = n * chunks
    own_rows = out.shape[0]
    h2, h4 = m // 2, m // 4
    slots = half.shape[0]
    partner = {"row": r + 1 - 2 * core}
    x_peer = {"row": y * 4 + (1 - x) * 2 + core}

    def y_peer(step):
        return {"row": ((y + step) % ny) * 4 + x * 2 + core}

    load_weight = pltpu.make_async_copy(weight_hbm, weight, load_sem.at[0])
    load_own = pltpu.make_async_copy(
        cot_hbm, gathered.at[pl.ds(0, shard)], load_sem.at[1]
    )
    load_own.start()
    load_weight.start()

    barrier = pltpu.get_barrier_semaphore()
    peers = [partner, x_peer] + [y_peer(k) for k in range(1, ny)]
    for peer in peers:
        pl.semaphore_signal(barrier, inc=1, device_id=peer, device_id_type=MESH)

    @pl.when(z > 0)
    def _():
        pl.semaphore_signal(barrier, inc=1, device_id={"col": z - 1}, device_id_type=MESH)

    @pl.when(z < n - 1)
    def _():
        pl.semaphore_signal(barrier, inc=1, device_id={"col": z + 1}, device_id_type=MESH)

    ends = jnp.where(z > 0, 1, 0) + jnp.where(z < n - 1, 1, 0)
    pl.semaphore_wait(barrier, len(peers) + ends)
    load_own.wait()

    def position(holder, s, c):
        pairs = jnp.minimum(holder, n - 1 - holder)
        distance = jnp.where(s > holder, s - holder, holder - s)
        near = jnp.where(s > holder, 2 * distance - 1, 2 * distance)
        p = jnp.where(distance <= pairs, near, pairs + distance)
        return jnp.where(s == holder, c, chunks + c * (n - 1) + p - 1)

    def rows_at(i):
        return pl.ds(pl.multiple_of(i * m, 16), m)

    def z_copy(s, c, side, target):
        return pltpu.make_async_remote_copy(
            src_ref=gathered.at[rows_at(position(z, s, c))],
            dst_ref=gathered.at[rows_at(position(target, s, c))],
            send_sem=zsend.at[side, s * chunks + c],
            recv_sem=zrecv.at[s * chunks + c],
            device_id={"col": target},
            device_id_type=MESH,
        )

    def pass_left(s, c):
        @pl.when(z > 0)
        def _():
            z_copy(s, c, 0, z - 1).start()

    def pass_right(s, c):
        @pl.when(z < n - 1)
        def _():
            z_copy(s, c, 1, z + 1).start()

    ahead = min(2, chunks)
    for c in range(ahead):
        pass_left(z, c)
        pass_right(z, c)

    pairs = jnp.minimum(z, n - 1 - z)

    def place(i):
        q = jnp.maximum(i - chunks, 0)
        c = jnp.where(i < chunks, i, q // (n - 1))
        p = jnp.where(i < chunks, 0, q % (n - 1) + 1)
        near = (p + 1) // 2
        near_shard = jnp.where(p % 2 == 1, z + near, z - near)
        far = p - pairs
        far_shard = jnp.where(z < n - 1 - z, z + far, z - far)
        s = jnp.where(p <= 2 * pairs, near_shard, far_shard)
        token = s * shard + c * m
        dest = token // own_rows
        return c, p, s, dest, token % own_rows

    def copy_core(slot, row):
        return pltpu.make_async_remote_copy(
            src_ref=part.at[pl.ds(pl.multiple_of(row + (1 - core) * h2, 8), h2)],
            dst_ref=core_in.at[slot],
            send_sem=core_send.at[slot],
            recv_sem=core_recv.at[slot],
            device_id=partner,
            device_id_type=MESH,
        )

    def copy_quarter(slot, q, landing, target):
        return pltpu.make_async_remote_copy(
            src_ref=half.at[slot, pl.ds(q * h4, h4)],
            dst_ref=arrive.at[slot, landing],
            send_sem=quarter_send.at[slot, q],
            recv_sem=arrive_sem.at[slot, landing],
            device_id=target,
            device_id_type=MESH,
        )

    def first_hop(slot, dest):
        yd, xd = dest // 4, (dest // 2) % 2

        @pl.when(y != yd)
        def _():
            landing = 2 + (y - yd + ny) % ny - 1
            copy_quarter(slot, 0, landing, {"row": yd * 4 + x * 2 + core}).start()

        @pl.when(x != xd)
        def _():
            copy_quarter(slot, 1, 0, x_peer).start()

    def wait_landing(slot, landing):
        copy_quarter(slot, 0, landing, x_peer).wait_recv()

    def second_hop(i):
        _, _, _, dest, _ = place(i)
        slot = i % slots
        yd, xd = dest // 4, (dest // 2) % 2

        @pl.when(y == yd)
        def _():
            for k in range(ny - 1):
                wait_landing(slot, 2 + k)
                half[slot, pl.ds(0, h4)] += arrive[slot, 2 + k]

            @pl.when(x != xd)
            def _():
                copy_quarter(slot, 0, 1, x_peer).start()

        @pl.when(x == xd)
        def _():
            wait_landing(slot, 0)
            half[slot, pl.ds(h4, h4)] += arrive[slot, 0]

            @pl.when(y != yd)
            def _():
                landing = 2 + ny - 1 + (y - yd + ny) % ny - 1
                copy_quarter(slot, 1, landing, {"row": yd * 4 + x * 2 + core}).start()

    def fin_copy(start, index):
        return pltpu.make_async_remote_copy(
            src_ref=fin,
            dst_ref=out.at[pl.ds(pl.multiple_of(start, 16), h2)],
            send_sem=fin_send.at[0],
            recv_sem=fin_recv.at[index],
            device_id=partner,
            device_id_type=MESH,
        )

    def finish(i):
        _, _, _, dest, local = place(i)
        slot = i % slots
        yd, xd, cored = dest // 4, (dest // 2) % 2, dest % 2
        here = jnp.logical_and(y == yd, x == xd)

        @pl.when(here)
        def _():
            wait_landing(slot, 1)
            half[slot, pl.ds(0, h4)] += arrive[slot, 1]
            for k in range(ny - 1):
                wait_landing(slot, 2 + ny - 1 + k)
                half[slot, pl.ds(h4, h4)] += arrive[slot, 2 + ny - 1 + k]
            start = local + core * h2

            @pl.when(core == cored)
            def _():
                out[pl.ds(pl.multiple_of(start, 16), h2)] = half[slot].astype(jnp.bfloat16)

            @pl.when(core != cored)
            def _():
                fin[...] = half[slot].astype(jnp.bfloat16)
                copy = fin_copy(start, local // m)
                copy.start()
                copy.wait_send()

        @pl.when(jnp.logical_not(here))
        def _():
            copy_quarter(slot, 0, 0, x_peer).wait_send()
            copy_quarter(slot, 1, 0, x_peer).wait_send()

        @pl.when(i < total - slots)
        def _():
            for k, peer in enumerate(peers):
                index = k if k < 2 else 2 + (ny - (k - 1)) - 1
                pl.semaphore_signal(credit.at[index], inc=1, device_id=peer, device_id_type=MESH)

    block = min(256, width)
    whole_blocks = width // block

    def multiply(first, count):
        size = count * m
        lhs = pl.ds(first * m, size)
        rank = up3.shape[0] // 3
        low = contract_trailing_axis(gathered[lhs], up3[...])
        high = low.astype(jnp.bfloat16)
        rest = low - high.astype(jnp.float32)
        middle = rest.astype(jnp.bfloat16)
        last = (rest - middle.astype(jnp.float32)).astype(jnp.bfloat16)
        lane = lax.broadcasted_iota(jnp.int32, low.shape, 1)
        split = jnp.where(
            lane < rank,
            high.astype(jnp.float32),
            jnp.where(lane < 2 * rank, middle.astype(jnp.float32), last.astype(jnp.float32)),
        ).astype(jnp.bfloat16)

        def columns(start, extent):
            value = contract_trailing_axis(gathered[lhs], weight[pl.ds(start, extent)])
            part[pl.ds(0, size), pl.ds(start, extent)] = value + contract_trailing_axis(
                split, down3[pl.ds(start, extent)]
            )

        @pl.loop(0, whole_blocks)
        def _(j):
            columns(pl.multiple_of(j * block, block), block)

        if width % block:
            columns(whole_blocks * block, width % block)

    def receive(i):
        c, p, s, _, _ = place(i)

        @pl.when(jnp.logical_and(p == 1, c + ahead < chunks))
        def _():
            pass_left(z, c + ahead)
            pass_right(z, c + ahead)

        z_copy(s, c, 0, z).wait_recv()

        @pl.when(s > z)
        def _():
            pass_left(s, c)

        @pl.when(s < z)
        def _():
            pass_right(s, c)

    previous = None
    for first, count in batches:
        if first >= chunks:
            pl.loop(first, first + count)(receive)
        if previous is not None:
            pl.loop(previous[0], sum(previous))(second_hop)
        if first == 0:
            load_weight.wait()
        multiply(first, count)
        if previous is not None:
            pl.loop(previous[0], sum(previous))(finish)

        @pl.loop(first, first + count)
        def _(i):
            @pl.when(i >= slots)
            def _():
                for k in range(len(peers)):
                    pl.semaphore_wait(credit.at[k], 1)

            copy_core(i % slots, (i - first) * m).start()

        @pl.loop(first, first + count)
        def _(i):
            _, _, _, dest, _ = place(i)
            slot = i % slots
            row = (i - first) * m
            copy_core(slot, row).wait()
            own = pl.ds(pl.multiple_of(row + core * h2, 8), h2)
            half[slot] = part[own] + core_in[slot]
            first_hop(slot, dest)

        previous = (first, count)

    pl.loop(previous[0], sum(previous))(second_hop)
    pl.loop(previous[0], sum(previous))(finish)

    for index in range(own_rows // m):
        fin_copy(index * m, index).wait_recv()

    @pl.loop(0, total)
    def _(i):
        c, _, s, _, _ = place(i)

        @pl.when(jnp.logical_and(z > 0, s >= z))
        def _():
            z_copy(s, c, 0, z).wait_send()

        @pl.when(jnp.logical_and(z < n - 1, s <= z))
        def _():
            z_copy(s, c, 1, z).wait_send()


def plan(n, chunks):
    batches = [(0, chunks)]
    first, end = chunks, chunks * n
    while first < end:
        count = n if first == chunks else n - 1
        batches.append((first, min(count, end - first)))
        first += count
    return tuple(batches)


def input_gradient(n, rows, cotangent, weight, up_slice, down_slice):
    shard, hidden = cotangent.shape
    width = weight.shape[0]
    tokens = shard * n
    m = CHUNK
    total = tokens // m
    ny = rows // 4
    own_rows = tokens // rows
    batches = plan(n, shard // m)
    slots = max(count for _, count in batches)
    up3 = jnp.concatenate([up_slice] * 3, axis=0)
    down3 = jnp.concatenate([down_slice * jnp.bfloat16(scaling)] * 3, axis=1)
    vmem = pl.BlockSpec(memory_space=pltpu.VMEM)
    hbm = pl.BlockSpec(memory_space=pl.ANY)
    return pl.pallas_call(
        functools.partial(input_gradient_kernel, n, rows, batches),
        out_shape=jax.ShapeDtypeStruct((own_rows, width), jnp.bfloat16),
        in_specs=[hbm, hbm, vmem, vmem],
        out_specs=vmem,
        scratch_shapes=[
            pltpu.VMEM((tokens, hidden), jnp.bfloat16),
            pltpu.VMEM((width, hidden), jnp.bfloat16),
            pltpu.VMEM((slots * m, width), jnp.float32),
            pltpu.VMEM((slots, m // 2, width), jnp.float32),
            pltpu.VMEM((slots, m // 2, width), jnp.float32),
            pltpu.VMEM((slots, 2 * ny, m // 4, width), jnp.float32),
            pltpu.VMEM((m // 2, width), jnp.bfloat16),
            pltpu.SemaphoreType.DMA((2,)),
            pltpu.SemaphoreType.DMA((2, total)),
            pltpu.SemaphoreType.DMA((total,)),
            pltpu.SemaphoreType.DMA((slots,)),
            pltpu.SemaphoreType.DMA((slots,)),
            pltpu.SemaphoreType.DMA((slots, 2)),
            pltpu.SemaphoreType.DMA((slots, 2 * ny)),
            pltpu.SemaphoreType.DMA((1,)),
            pltpu.SemaphoreType.DMA((own_rows // m,)),
            pltpu.SemaphoreType.REGULAR((ny + 1,)),
        ],
        compiler_params=pltpu.CompilerParams(
            collective_id=0, has_side_effects=True, vmem_limit_bytes=62 * 2**20
        ),
        cost_estimate=pl.CostEstimate(
            flops=2 * tokens * width * hidden,
            bytes_accessed=2 * width * hidden,
            transcendentals=0,
        ),
        name="input_gradient",
    )(cotangent, weight, up3, down3)


def on_device(n, rows, inputs, cotangent, weight, adapter_down_factor, adapter_up_factor):
    row_position = lax.axis_index("row")
    column_position = lax.axis_index("col")
    width_row_block = inputs.shape[1]
    width_columns = weight.shape[0]
    hidden_columns = cotangent.shape[1]
    down_factor_rows = lax.dynamic_slice_in_dim(
        adapter_down_factor, row_position * width_row_block, width_row_block, 0
    )
    down_factor_columns = lax.dynamic_slice_in_dim(
        adapter_down_factor, column_position * width_columns, width_columns, 0
    )
    up_weight_slice = lax.dynamic_slice_in_dim(
        adapter_up_factor, row_position * hidden_columns, hidden_columns, 1
    )
    grad_input = input_gradient(
        n, rows, cotangent, weight, up_weight_slice, down_factor_columns
    )
    low_part = contract_trailing_axis(cotangent, up_weight_slice)
    proj_part = jnp.dot(inputs, down_factor_rows, preferred_element_type=jnp.float32)
    gradient_lowrank, projected_rows = lax.psum((low_part, proj_part), "row")
    part_a = scaling * jnp.dot(
        inputs.astype(jnp.float32).T, gradient_lowrank, precision=lax.Precision.HIGHEST
    )
    part_b = scaling * jnp.dot(
        projected_rows.T, cotangent.astype(jnp.float32), precision=lax.Precision.HIGHEST
    )
    grad_a, grad_b = lax.psum((part_a, part_b), "col")
    return (grad_input, grad_a, grad_b)


def solution(mesh):
    in_specs = (P("col", "row"), P("col", "row"), P("col", "row"), P(), P())
    out_specs = (P("row", "col"), P("row", None), P(None, "row"))
    body = functools.partial(on_device, mesh.shape["col"], mesh.shape["row"])
    return jax.shard_map(
        body, mesh=mesh, in_specs=in_specs, out_specs=out_specs, check_vma=False
    )
```

```python
import functools

import jax
import jax.numpy as jnp
from jax import lax
from jax.experimental import pallas as pl
from jax.experimental.pallas import tpu as pltpu
from jax.sharding import PartitionSpec as P

scaling = 2.0
MESH = pl.DeviceIdType.MESH
CHUNK = 64


def contract_trailing_axis(left, right):
    return lax.dot_general(
        left, right, (((1,), (1,)), ((), ())), preferred_element_type=jnp.float32
    )


def input_gradient_kernel(
    n, rows, batches, cot_hbm, weight_hbm, up3, down3, inputs, down_rows, out, grad_a, grad_b,
    gathered, weight, part, core_in, half, arrive, fin,
    load_sem, zsend, zrecv, core_send, core_recv, quarter_send, arrive_sem,
    fin_send, fin_recv, credit,
    small, proj, proj_split, chain, chain_in, small_send, small_recv, proj_send, proj_recv,
    chain_send, chain_recv, spread_send, spread_recv,
):
    z = lax.axis_index("col")
    r = lax.axis_index("row")
    core = r % 2
    x = (r // 2) % 2
    y = r // 4
    ny = rows // 4
    shard = cot_hbm.shape[0]
    width = weight_hbm.shape[0]
    m = CHUNK
    chunks = shard // m
    total = n * chunks
    own_rows = out.shape[0]
    h2, h4 = m // 2, m // 4
    slots = half.shape[0]
    partner = {"row": r + 1 - 2 * core}
    x_peer = {"row": y * 4 + (1 - x) * 2 + core}

    def y_peer(step):
        return {"row": ((y + step) % ny) * 4 + x * 2 + core}

    load_weight = pltpu.make_async_copy(weight_hbm, weight, load_sem.at[0])
    load_own = pltpu.make_async_copy(
        cot_hbm, gathered.at[pl.ds(0, shard)], load_sem.at[1]
    )
    load_own.start()
    load_weight.start()

    barrier = pltpu.get_barrier_semaphore()
    peers = [partner, x_peer] + [y_peer(k) for k in range(1, ny)]
    row_peers = [{"row": (r + k) % rows} for k in range(1, rows)]
    col_peers = [{"col": (z + k) % n} for k in range(1, n)]
    for peer in row_peers + col_peers:
        pl.semaphore_signal(barrier, inc=1, device_id=peer, device_id_type=MESH)
    pl.semaphore_wait(barrier, rows - 1 + n - 1)
    load_own.wait()

    def position(holder, s, c):
        pairs = jnp.minimum(holder, n - 1 - holder)
        distance = jnp.where(s > holder, s - holder, holder - s)
        near = jnp.where(s > holder, 2 * distance - 1, 2 * distance)
        p = jnp.where(distance <= pairs, near, pairs + distance)
        return jnp.where(s == holder, c, chunks + c * (n - 1) + p - 1)

    def rows_at(i):
        return pl.ds(pl.multiple_of(i * m, 16), m)

    def z_copy(s, c, side, target):
        return pltpu.make_async_remote_copy(
            src_ref=gathered.at[rows_at(position(z, s, c))],
            dst_ref=gathered.at[rows_at(position(target, s, c))],
            send_sem=zsend.at[side, s * chunks + c],
            recv_sem=zrecv.at[s * chunks + c],
            device_id={"col": target},
            device_id_type=MESH,
        )

    def pass_left(s, c):
        @pl.when(z > 0)
        def _():
            z_copy(s, c, 0, z - 1).start()

    def pass_right(s, c):
        @pl.when(z < n - 1)
        def _():
            z_copy(s, c, 1, z + 1).start()

    ahead = min(2, chunks)
    for c in range(ahead):
        pass_left(z, c)
        pass_right(z, c)

    pairs = jnp.minimum(z, n - 1 - z)

    def place(i):
        q = jnp.maximum(i - chunks, 0)
        c = jnp.where(i < chunks, i, q // (n - 1))
        p = jnp.where(i < chunks, 0, q % (n - 1) + 1)
        near = (p + 1) // 2
        near_shard = jnp.where(p % 2 == 1, z + near, z - near)
        far = p - pairs
        far_shard = jnp.where(z < n - 1 - z, z + far, z - far)
        s = jnp.where(p <= 2 * pairs, near_shard, far_shard)
        token = s * shard + c * m
        dest = token // own_rows
        return c, p, s, dest, token % own_rows

    def copy_core(slot, row):
        return pltpu.make_async_remote_copy(
            src_ref=part.at[pl.ds(pl.multiple_of(row + (1 - core) * h2, 8), h2)],
            dst_ref=core_in.at[slot],
            send_sem=core_send.at[slot],
            recv_sem=core_recv.at[slot],
            device_id=partner,
            device_id_type=MESH,
        )

    def copy_quarter(slot, q, landing, target):
        return pltpu.make_async_remote_copy(
            src_ref=half.at[slot, pl.ds(q * h4, h4)],
            dst_ref=arrive.at[slot, landing],
            send_sem=quarter_send.at[slot, q],
            recv_sem=arrive_sem.at[slot, landing],
            device_id=target,
            device_id_type=MESH,
        )

    def first_hop(slot, dest):
        yd, xd = dest // 4, (dest // 2) % 2

        @pl.when(y != yd)
        def _():
            landing = 2 + (y - yd + ny) % ny - 1
            copy_quarter(slot, 0, landing, {"row": yd * 4 + x * 2 + core}).start()

        @pl.when(x != xd)
        def _():
            copy_quarter(slot, 1, 0, x_peer).start()

    def wait_landing(slot, landing):
        copy_quarter(slot, 0, landing, x_peer).wait_recv()

    def second_hop(i):
        _, _, _, dest, _ = place(i)
        slot = i % slots
        yd, xd = dest // 4, (dest // 2) % 2

        @pl.when(y == yd)
        def _():
            for k in range(ny - 1):
                wait_landing(slot, 2 + k)
                half[slot, pl.ds(0, h4)] += arrive[slot, 2 + k]

            @pl.when(x != xd)
            def _():
                copy_quarter(slot, 0, 1, x_peer).start()

        @pl.when(x == xd)
        def _():
            wait_landing(slot, 0)
            half[slot, pl.ds(h4, h4)] += arrive[slot, 0]

            @pl.when(y != yd)
            def _():
                landing = 2 + ny - 1 + (y - yd + ny) % ny - 1
                copy_quarter(slot, 1, landing, {"row": yd * 4 + x * 2 + core}).start()

    def fin_copy(start, index):
        return pltpu.make_async_remote_copy(
            src_ref=fin,
            dst_ref=out.at[pl.ds(pl.multiple_of(start, 16), h2)],
            send_sem=fin_send.at[0],
            recv_sem=fin_recv.at[index],
            device_id=partner,
            device_id_type=MESH,
        )

    def finish(i):
        _, _, _, dest, local = place(i)
        slot = i % slots
        yd, xd, cored = dest // 4, (dest // 2) % 2, dest % 2
        here = jnp.logical_and(y == yd, x == xd)

        @pl.when(here)
        def _():
            wait_landing(slot, 1)
            half[slot, pl.ds(0, h4)] += arrive[slot, 1]
            for k in range(ny - 1):
                wait_landing(slot, 2 + ny - 1 + k)
                half[slot, pl.ds(h4, h4)] += arrive[slot, 2 + ny - 1 + k]
            start = local + core * h2

            @pl.when(core == cored)
            def _():
                out[pl.ds(pl.multiple_of(start, 16), h2)] = half[slot].astype(jnp.bfloat16)

            @pl.when(core != cored)
            def _():
                fin[...] = half[slot].astype(jnp.bfloat16)
                copy = fin_copy(start, local // m)
                copy.start()
                copy.wait_send()

        @pl.when(jnp.logical_not(here))
        def _():
            copy_quarter(slot, 0, 0, x_peer).wait_send()
            copy_quarter(slot, 1, 0, x_peer).wait_send()

        @pl.when(i < total - slots)
        def _():
            for k, peer in enumerate(peers):
                index = k if k < 2 else 2 + (ny - (k - 1)) - 1
                pl.semaphore_signal(credit.at[index], inc=1, device_id=peer, device_id_type=MESH)

    block = min(256, width)
    whole_blocks = width // block

    inner = jnp.logical_and(z > 0, z < n - 1)

    def multiply(first, count, coming):
        size = count * m
        lhs = pl.ds(first * m, size)
        rank = up3.shape[0] // 3
        low = contract_trailing_axis(gathered[lhs], up3[...])
        high = low.astype(jnp.bfloat16)
        rest = low - high.astype(jnp.float32)
        middle = rest.astype(jnp.bfloat16)
        last = (rest - middle.astype(jnp.float32)).astype(jnp.bfloat16)
        lane = lax.broadcasted_iota(jnp.int32, low.shape, 1)
        split = jnp.where(
            lane < rank,
            high.astype(jnp.float32),
            jnp.where(lane < 2 * rank, middle.astype(jnp.float32), last.astype(jnp.float32)),
        ).astype(jnp.bfloat16)

        def columns(start, extent):
            value = contract_trailing_axis(gathered[lhs], weight[pl.ds(start, extent)])
            part[pl.ds(0, size), pl.ds(start, extent)] = value + contract_trailing_axis(
                split, down3[pl.ds(start, extent)]
            )

        parts = max(1, coming[1])
        for k in range(parts):
            if k < coming[1]:
                pl.when(inner)(functools.partial(receive, coming[0] + k))

            @pl.loop(whole_blocks * k // parts, whole_blocks * (k + 1) // parts)
            def _(j):
                columns(pl.multiple_of(j * block, block), block)

        if width % block:
            columns(whole_blocks * block, width % block)

    def receive(i):
        c, p, s, _, _ = place(i)

        @pl.when(jnp.logical_and(p == 1, c + ahead < chunks))
        def _():
            pass_left(z, c + ahead)
            pass_right(z, c + ahead)

        z_copy(s, c, 0, z).wait_recv()

        @pl.when(s > z)
        def _():
            pass_left(s, c)

        @pl.when(s < z)
        def _():
            pass_right(s, c)

    rank = up3.shape[0] // 3

    def pieces(value):
        high = value.astype(jnp.bfloat16)
        rest = value - high.astype(jnp.float32)
        middle = rest.astype(jnp.bfloat16)
        last = (rest - middle.astype(jnp.float32)).astype(jnp.bfloat16)
        return jnp.concatenate([high, middle, last], axis=0)

    def folded(value):
        return scaling * (value[:rank] + value[rank : 2 * rank] + value[2 * rank :])

    def small_copy(k):
        return pltpu.make_async_remote_copy(
            src_ref=small.at[r], dst_ref=small.at[r],
            send_sem=small_send.at[k - 1], recv_sem=small_recv.at[r],
            device_id=row_peers[k - 1], device_id_type=MESH,
        )

    def proj_copy(k):
        return pltpu.make_async_remote_copy(
            src_ref=proj.at[z], dst_ref=proj.at[z],
            send_sem=proj_send.at[k - 1], recv_sem=proj_recv.at[z],
            device_id=col_peers[k - 1], device_id_type=MESH,
        )

    def chain_copy():
        return pltpu.make_async_remote_copy(
            src_ref=chain, dst_ref=chain_in,
            send_sem=chain_send.at[0], recv_sem=chain_recv.at[0],
            device_id={"col": (z + 1) % n}, device_id_type=MESH,
        )

    def spread_copy(k):
        return pltpu.make_async_remote_copy(
            src_ref=grad_a, dst_ref=grad_a,
            send_sem=spread_send.at[k - 1], recv_sem=spread_recv.at[0],
            device_id=col_peers[k - 1], device_id_type=MESH,
        )

    def send_small():
        for c in range(chunks):
            own = pl.ds(c * m, m)
            small[r, c, pl.ds(0, rank)] = contract_trailing_axis(up3[pl.ds(0, rank)], gathered[own])
            small[r, c, pl.ds(rank, rank)] = contract_trailing_axis(down_rows[...], inputs[own])
        for k in range(1, rows):
            small_copy(k).start()

    def use_small():
        for k in range(1, rows):
            other = (r + k) % rows
            pltpu.make_async_remote_copy(
                src_ref=small.at[other], dst_ref=small.at[other],
                send_sem=small_send.at[0], recv_sem=small_recv.at[other],
                device_id=row_peers[0], device_id_type=MESH,
            ).wait_recv()
        for c in range(chunks):
            value = small[0, c]
            for q in range(1, rows):
                value = value + small[q, c]
            proj[z, c] = value[rank:]
            term = folded(
                jnp.dot(
                    pieces(value[:rank]), inputs[pl.ds(c * m, m)],
                    preferred_element_type=jnp.float32,
                )
            )
            chain[...] = term if c == 0 else chain[...] + term
        for k in range(1, n):
            proj_copy(k).start()

    def advance_chain():
        @pl.when(z > 0)
        def _():
            chain_copy().wait_recv()
            chain[...] += chain_in[...]

        @pl.when(z < n - 1)
        def _():
            chain_copy().start()

        @pl.when(z == n - 1)
        def _():
            grad_a[...] = chain[...]
            for k in range(1, n):
                spread_copy(k).start()

    def up_gradient():
        for k in range(1, n):
            other = (z + k) % n
            pltpu.make_async_remote_copy(
                src_ref=proj.at[other], dst_ref=proj.at[other],
                send_sem=proj_send.at[0], recv_sem=proj_recv.at[other],
                device_id=col_peers[0], device_id_type=MESH,
            ).wait_recv()

        @pl.loop(0, total)
        def _(i):
            c, _, s, _, _ = place(i)
            proj_split[i] = pieces(proj[s, c])

        hidden = grad_b.shape[1]
        step = 384 if hidden % 384 == 0 else hidden

        @pl.loop(0, hidden // step)
        def _(j):
            lanes = pl.ds(pl.multiple_of(j * step, 128), step)
            value = None
            for i in range(total):
                term = jnp.dot(
                    proj_split[i], gathered[pl.ds(i * m, m), lanes],
                    preferred_element_type=jnp.float32,
                )
                value = term if value is None else value + term
            grad_b[:, lanes] = folded(value)

    send_small()
    previous = None
    for turn, (first, count) in enumerate(batches):
        coming = batches[turn + 1] if turn + 1 < len(batches) else (0, 0)
        if first >= chunks:

            @pl.when(jnp.logical_not(inner))
            def _():
                pl.loop(first, first + count)(receive)

        if previous is not None:
            pl.loop(previous[0], sum(previous))(second_hop)
        if first == 0:
            load_weight.wait()
        multiply(first, count, coming)
        if previous is not None:
            pl.loop(previous[0], sum(previous))(finish)

        @pl.loop(first, first + count)
        def _(i):
            @pl.when(i >= slots)
            def _():
                for k in range(len(peers)):
                    pl.semaphore_wait(credit.at[k], 1)

            copy_core(i % slots, (i - first) * m).start()

        @pl.loop(first, first + count)
        def _(i):
            _, _, _, dest, _ = place(i)
            slot = i % slots
            row = (i - first) * m
            copy_core(slot, row).wait()
            own = pl.ds(pl.multiple_of(row + core * h2, 8), h2)
            half[slot] = part[own] + core_in[slot]
            first_hop(slot, dest)

        if turn == 0:
            use_small()
        if turn < chunks:
            pl.when(z * chunks // n == turn)(advance_chain)
        previous = (first, count)

    up_gradient()

    pl.loop(previous[0], sum(previous))(second_hop)
    pl.loop(previous[0], sum(previous))(finish)

    for k in range(1, rows):
        small_copy(k).wait_send()
    for k in range(1, n):
        proj_copy(k).wait_send()

    @pl.when(z < n - 1)
    def _():
        chain_copy().wait_send()
        spread_copy(1).wait_recv()

    @pl.when(z == n - 1)
    def _():
        for k in range(1, n):
            spread_copy(k).wait_send()

    for index in range(own_rows // m):
        fin_copy(index * m, index).wait_recv()

    @pl.loop(0, total)
    def _(i):
        c, _, s, _, _ = place(i)

        @pl.when(jnp.logical_and(z > 0, s >= z))
        def _():
            z_copy(s, c, 0, z).wait_send()

        @pl.when(jnp.logical_and(z < n - 1, s <= z))
        def _():
            z_copy(s, c, 1, z).wait_send()


def plan(n, chunks):
    batches = [(0, chunks)]
    first, end = chunks, chunks * n
    while first < end:
        count = n if first == chunks else n - 1
        batches.append((first, min(count, end - first)))
        first += count
    return tuple(batches)


def gradients(n, rows, inputs, cotangent, weight, up_slice, down_slice, down_rows):
    shard, hidden = cotangent.shape
    width = weight.shape[0]
    tokens = shard * n
    m = CHUNK
    total = tokens // m
    ny = rows // 4
    own_rows = tokens // rows
    batches = plan(n, shard // m)
    slots = max(count for _, count in batches)
    rank = up_slice.shape[0]
    chunks = shard // m
    up3 = jnp.concatenate([up_slice] * 3, axis=0)
    down3 = jnp.concatenate([down_slice * jnp.bfloat16(scaling)] * 3, axis=1)
    vmem = pl.BlockSpec(memory_space=pltpu.VMEM)
    hbm = pl.BlockSpec(memory_space=pl.ANY)
    return pl.pallas_call(
        functools.partial(input_gradient_kernel, n, rows, batches),
        out_shape=[
            jax.ShapeDtypeStruct((own_rows, width), jnp.bfloat16),
            jax.ShapeDtypeStruct((rank, inputs.shape[1]), jnp.float32),
            jax.ShapeDtypeStruct((rank, hidden), jnp.float32),
        ],
        in_specs=[hbm, hbm, vmem, vmem, vmem, vmem],
        out_specs=[vmem, vmem, vmem],
        scratch_shapes=[
            pltpu.VMEM((tokens, hidden), jnp.bfloat16),
            pltpu.VMEM((width, hidden), jnp.bfloat16),
            pltpu.VMEM((slots * m, width), jnp.float32),
            pltpu.VMEM((slots, m // 2, width), jnp.float32),
            pltpu.VMEM((slots, m // 2, width), jnp.float32),
            pltpu.VMEM((slots, 2 * ny, m // 4, width), jnp.float32),
            pltpu.VMEM((m // 2, width), jnp.bfloat16),
            pltpu.SemaphoreType.DMA((2,)),
            pltpu.SemaphoreType.DMA((2, total)),
            pltpu.SemaphoreType.DMA((total,)),
            pltpu.SemaphoreType.DMA((slots,)),
            pltpu.SemaphoreType.DMA((slots,)),
            pltpu.SemaphoreType.DMA((slots, 2)),
            pltpu.SemaphoreType.DMA((slots, 2 * ny)),
            pltpu.SemaphoreType.DMA((1,)),
            pltpu.SemaphoreType.DMA((own_rows // m,)),
            pltpu.SemaphoreType.REGULAR((ny + 1,)),
            pltpu.VMEM((rows, chunks, 2 * rank, m), jnp.float32),
            pltpu.VMEM((n, chunks, rank, m), jnp.float32),
            pltpu.VMEM((total, 3 * rank, m), jnp.bfloat16),
            pltpu.VMEM((rank, inputs.shape[1]), jnp.float32),
            pltpu.VMEM((rank, inputs.shape[1]), jnp.float32),
            pltpu.SemaphoreType.DMA((rows - 1,)),
            pltpu.SemaphoreType.DMA((rows,)),
            pltpu.SemaphoreType.DMA((n - 1,)),
            pltpu.SemaphoreType.DMA((n,)),
            pltpu.SemaphoreType.DMA((1,)),
            pltpu.SemaphoreType.DMA((1,)),
            pltpu.SemaphoreType.DMA((n - 1,)),
            pltpu.SemaphoreType.DMA((1,)),
        ],
        compiler_params=pltpu.CompilerParams(
            collective_id=0, has_side_effects=True, vmem_limit_bytes=62 * 2**20
        ),
        cost_estimate=pl.CostEstimate(
            flops=2 * tokens * width * hidden,
            bytes_accessed=2 * width * hidden,
            transcendentals=0,
        ),
        name="input_gradient",
    )(cotangent, weight, up3, down3, inputs, down_rows.T)


def on_device(n, rows, inputs, cotangent, weight, adapter_down_factor, adapter_up_factor):
    row_position = lax.axis_index("row")
    column_position = lax.axis_index("col")
    width_row_block = inputs.shape[1]
    width_columns = weight.shape[0]
    hidden_columns = cotangent.shape[1]
    down_factor_rows = lax.dynamic_slice_in_dim(
        adapter_down_factor, row_position * width_row_block, width_row_block, 0
    )
    down_factor_columns = lax.dynamic_slice_in_dim(
        adapter_down_factor, column_position * width_columns, width_columns, 0
    )
    up_weight_slice = lax.dynamic_slice_in_dim(
        adapter_up_factor, row_position * hidden_columns, hidden_columns, 1
    )
    grad_input, grad_a, grad_b = gradients(
        n, rows, inputs, cotangent, weight, up_weight_slice, down_factor_columns, down_factor_rows
    )
    grad_a = grad_a.T
    return (grad_input, grad_a, grad_b)


def solution(mesh):
    in_specs = (P("col", "row"), P("col", "row"), P("col", "row"), P(), P())
    out_specs = (P("row", "col"), P("row", None), P(None, "row"))
    body = functools.partial(on_device, mesh.shape["col"], mesh.shape["row"])
    return jax.shard_map(
        body, mesh=mesh, in_specs=in_specs, out_specs=out_specs, check_vma=False
    )
```

```python
import functools

import jax
import jax.numpy as jnp
from jax import lax
from jax.experimental import pallas as pl
from jax.experimental.pallas import tpu as pltpu
from jax.sharding import PartitionSpec as P

scaling = 2.0
MESH = pl.DeviceIdType.MESH
CHUNK = 64


def contract_trailing_axis(left, right):
    return lax.dot_general(
        left, right, (((1,), (1,)), ((), ())), preferred_element_type=jnp.float32
    )


def input_gradient_kernel(
    n, rows, batches, cot_hbm, weight_hbm, up3, down3, out,
    gathered, weight, part, core_in, half, arrive, fin,
    load_sem, zsend, zrecv, core_send, core_recv, quarter_send, arrive_sem,
    fin_send, fin_recv, credit,
):
    z = lax.axis_index("col")
    r = lax.axis_index("row")
    core = r % 2
    x = (r // 2) % 2
    y = r // 4
    ny = rows // 4
    shard = cot_hbm.shape[0]
    width = weight_hbm.shape[0]
    m = CHUNK
    chunks = shard // m
    total = n * chunks
    own_rows = out.shape[0]
    h2, h4 = m // 2, m // 4
    slots = half.shape[0]
    partner = {"row": r + 1 - 2 * core}
    x_peer = {"row": y * 4 + (1 - x) * 2 + core}

    def y_peer(step):
        return {"row": ((y + step) % ny) * 4 + x * 2 + core}

    load_weight = pltpu.make_async_copy(weight_hbm, weight, load_sem.at[0])
    load_own = pltpu.make_async_copy(
        cot_hbm, gathered.at[pl.ds(0, shard)], load_sem.at[1]
    )
    load_own.start()
    load_weight.start()

    barrier = pltpu.get_barrier_semaphore()
    peers = [partner, x_peer] + [y_peer(k) for k in range(1, ny)]
    for peer in peers:
        pl.semaphore_signal(barrier, inc=1, device_id=peer, device_id_type=MESH)

    @pl.when(z > 0)
    def _():
        pl.semaphore_signal(barrier, inc=1, device_id={"col": z - 1}, device_id_type=MESH)

    @pl.when(z < n - 1)
    def _():
        pl.semaphore_signal(barrier, inc=1, device_id={"col": z + 1}, device_id_type=MESH)

    ends = jnp.where(z > 0, 1, 0) + jnp.where(z < n - 1, 1, 0)
    pl.semaphore_wait(barrier, len(peers) + ends)
    load_own.wait()

    def position(holder, s, c):
        pairs = jnp.minimum(holder, n - 1 - holder)
        distance = jnp.where(s > holder, s - holder, holder - s)
        near = jnp.where(s > holder, 2 * distance - 1, 2 * distance)
        p = jnp.where(distance <= pairs, near, pairs + distance)
        return jnp.where(s == holder, c, chunks + c * (n - 1) + p - 1)

    def rows_at(i):
        return pl.ds(pl.multiple_of(i * m, 16), m)

    def z_copy(s, c, side, target):
        return pltpu.make_async_remote_copy(
            src_ref=gathered.at[rows_at(position(z, s, c))],
            dst_ref=gathered.at[rows_at(position(target, s, c))],
            send_sem=zsend.at[side, s * chunks + c],
            recv_sem=zrecv.at[s * chunks + c],
            device_id={"col": target},
            device_id_type=MESH,
        )

    def pass_left(s, c):
        @pl.when(z > 0)
        def _():
            z_copy(s, c, 0, z - 1).start()

    def pass_right(s, c):
        @pl.when(z < n - 1)
        def _():
            z_copy(s, c, 1, z + 1).start()

    ahead = min(2, chunks)
    for c in range(ahead):
        pass_left(z, c)
        pass_right(z, c)

    pairs = jnp.minimum(z, n - 1 - z)

    def place(i):
        q = jnp.maximum(i - chunks, 0)
        c = jnp.where(i < chunks, i, q // (n - 1))
        p = jnp.where(i < chunks, 0, q % (n - 1) + 1)
        near = (p + 1) // 2
        near_shard = jnp.where(p % 2 == 1, z + near, z - near)
        far = p - pairs
        far_shard = jnp.where(z < n - 1 - z, z + far, z - far)
        s = jnp.where(p <= 2 * pairs, near_shard, far_shard)
        token = s * shard + c * m
        dest = token // own_rows
        return c, p, s, dest, token % own_rows

    def copy_core(slot, row):
        return pltpu.make_async_remote_copy(
            src_ref=part.at[pl.ds(pl.multiple_of(row + (1 - core) * h2, 8), h2)],
            dst_ref=core_in.at[slot],
            send_sem=core_send.at[slot],
            recv_sem=core_recv.at[slot],
            device_id=partner,
            device_id_type=MESH,
        )

    def copy_quarter(slot, q, landing, target):
        return pltpu.make_async_remote_copy(
            src_ref=half.at[slot, pl.ds(q * h4, h4)],
            dst_ref=arrive.at[slot, landing],
            send_sem=quarter_send.at[slot, q],
            recv_sem=arrive_sem.at[slot, landing],
            device_id=target,
            device_id_type=MESH,
        )

    def first_hop(slot, dest):
        yd, xd = dest // 4, (dest // 2) % 2

        @pl.when(y != yd)
        def _():
            landing = 2 + (y - yd + ny) % ny - 1
            copy_quarter(slot, 0, landing, {"row": yd * 4 + x * 2 + core}).start()

        @pl.when(x != xd)
        def _():
            copy_quarter(slot, 1, 0, x_peer).start()

    def wait_landing(slot, landing):
        copy_quarter(slot, 0, landing, x_peer).wait_recv()

    def second_hop(i):
        _, _, _, dest, _ = place(i)
        slot = i % slots
        yd, xd = dest // 4, (dest // 2) % 2

        @pl.when(y == yd)
        def _():
            for k in range(ny - 1):
                wait_landing(slot, 2 + k)
                half[slot, pl.ds(0, h4)] += arrive[slot, 2 + k]

            @pl.when(x != xd)
            def _():
                copy_quarter(slot, 0, 1, x_peer).start()

        @pl.when(x == xd)
        def _():
            wait_landing(slot, 0)
            half[slot, pl.ds(h4, h4)] += arrive[slot, 0]

            @pl.when(y != yd)
            def _():
                landing = 2 + ny - 1 + (y - yd + ny) % ny - 1
                copy_quarter(slot, 1, landing, {"row": yd * 4 + x * 2 + core}).start()

    def fin_copy(start, index):
        return pltpu.make_async_remote_copy(
            src_ref=fin,
            dst_ref=out.at[pl.ds(pl.multiple_of(start, 16), h2)],
            send_sem=fin_send.at[0],
            recv_sem=fin_recv.at[index],
            device_id=partner,
            device_id_type=MESH,
        )

    def finish(i):
        _, _, _, dest, local = place(i)
        slot = i % slots
        yd, xd, cored = dest // 4, (dest // 2) % 2, dest % 2
        here = jnp.logical_and(y == yd, x == xd)

        @pl.when(here)
        def _():
            wait_landing(slot, 1)
            half[slot, pl.ds(0, h4)] += arrive[slot, 1]
            for k in range(ny - 1):
                wait_landing(slot, 2 + ny - 1 + k)
                half[slot, pl.ds(h4, h4)] += arrive[slot, 2 + ny - 1 + k]
            start = local + core * h2

            @pl.when(core == cored)
            def _():
                out[pl.ds(pl.multiple_of(start, 16), h2)] = half[slot].astype(jnp.bfloat16)

            @pl.when(core != cored)
            def _():
                fin[...] = half[slot].astype(jnp.bfloat16)
                copy = fin_copy(start, local // m)
                copy.start()
                copy.wait_send()

        @pl.when(jnp.logical_not(here))
        def _():
            copy_quarter(slot, 0, 0, x_peer).wait_send()
            copy_quarter(slot, 1, 0, x_peer).wait_send()

        @pl.when(i < total - slots)
        def _():
            for k, peer in enumerate(peers):
                index = k if k < 2 else 2 + (ny - (k - 1)) - 1
                pl.semaphore_signal(credit.at[index], inc=1, device_id=peer, device_id_type=MESH)

    block = min(256, width)
    whole_blocks = width // block

    def multiply(first, count):
        size = count * m
        lhs = pl.ds(first * m, size)
        rank = up3.shape[0] // 3
        low = contract_trailing_axis(gathered[lhs], up3[...])
        high = low.astype(jnp.bfloat16)
        rest = low - high.astype(jnp.float32)
        middle = rest.astype(jnp.bfloat16)
        last = (rest - middle.astype(jnp.float32)).astype(jnp.bfloat16)
        lane = lax.broadcasted_iota(jnp.int32, low.shape, 1)
        split = jnp.where(
            lane < rank,
            high.astype(jnp.float32),
            jnp.where(lane < 2 * rank, middle.astype(jnp.float32), last.astype(jnp.float32)),
        ).astype(jnp.bfloat16)

        def columns(start, extent):
            for top in range(0, size, 2 * m):
                height = min(2 * m, size - top)
                value = contract_trailing_axis(
                    gathered[pl.ds(first * m + top, height)], weight[pl.ds(start, extent)]
                )
                part[pl.ds(top, height), pl.ds(start, extent)] = value + contract_trailing_axis(
                    split[top : top + height], down3[pl.ds(start, extent)]
                )

        @pl.loop(0, whole_blocks)
        def _(j):
            columns(pl.multiple_of(j * block, block), block)

        if width % block:
            columns(whole_blocks * block, width % block)

    def receive(i):
        c, p, s, _, _ = place(i)

        @pl.when(jnp.logical_and(p == 1, c + ahead < chunks))
        def _():
            pass_left(z, c + ahead)
            pass_right(z, c + ahead)

        z_copy(s, c, 0, z).wait_recv()

        @pl.when(s > z)
        def _():
            pass_left(s, c)

        @pl.when(s < z)
        def _():
            pass_right(s, c)

    previous = None
    for first, count in batches:
        if first >= chunks:
            pl.loop(first, first + count)(receive)
        if previous is not None:
            pl.loop(previous[0], sum(previous))(second_hop)
        if first == 0:
            load_weight.wait()
        multiply(first, count)
        if previous is not None:
            pl.loop(previous[0], sum(previous))(finish)

        @pl.loop(first, first + count)
        def _(i):
            @pl.when(i >= slots)
            def _():
                for k in range(len(peers)):
                    pl.semaphore_wait(credit.at[k], 1)

            copy_core(i % slots, (i - first) * m).start()

        @pl.loop(first, first + count)
        def _(i):
            _, _, _, dest, _ = place(i)
            slot = i % slots
            row = (i - first) * m
            copy_core(slot, row).wait()
            own = pl.ds(pl.multiple_of(row + core * h2, 8), h2)
            half[slot] = part[own] + core_in[slot]
            first_hop(slot, dest)

        previous = (first, count)

    pl.loop(previous[0], sum(previous))(second_hop)
    pl.loop(previous[0], sum(previous))(finish)

    for index in range(own_rows // m):
        fin_copy(index * m, index).wait_recv()

    @pl.loop(0, total)
    def _(i):
        c, _, s, _, _ = place(i)

        @pl.when(jnp.logical_and(z > 0, s >= z))
        def _():
            z_copy(s, c, 0, z).wait_send()

        @pl.when(jnp.logical_and(z < n - 1, s <= z))
        def _():
            z_copy(s, c, 1, z).wait_send()


def plan(n, chunks):
    batches = [(0, chunks)]
    first, end = chunks, chunks * n
    while first < end:
        count = n if first == chunks else n - 1
        batches.append((first, min(count, end - first)))
        first += count
    return tuple(batches)


def input_gradient(n, rows, cotangent, weight, up_slice, down_slice):
    shard, hidden = cotangent.shape
    width = weight.shape[0]
    tokens = shard * n
    m = CHUNK
    total = tokens // m
    ny = rows // 4
    own_rows = tokens // rows
    batches = plan(n, shard // m)
    slots = max(count for _, count in batches)
    up3 = jnp.concatenate([up_slice] * 3, axis=0)
    down3 = jnp.concatenate([down_slice * jnp.bfloat16(scaling)] * 3, axis=1)
    vmem = pl.BlockSpec(memory_space=pltpu.VMEM)
    hbm = pl.BlockSpec(memory_space=pl.ANY)
    return pl.pallas_call(
        functools.partial(input_gradient_kernel, n, rows, batches),
        out_shape=jax.ShapeDtypeStruct((own_rows, width), jnp.bfloat16),
        in_specs=[hbm, hbm, vmem, vmem],
        out_specs=vmem,
        scratch_shapes=[
            pltpu.VMEM((tokens, hidden), jnp.bfloat16),
            pltpu.VMEM((width, hidden), jnp.bfloat16),
            pltpu.VMEM((slots * m, width), jnp.float32),
            pltpu.VMEM((slots, m // 2, width), jnp.float32),
            pltpu.VMEM((slots, m // 2, width), jnp.float32),
            pltpu.VMEM((slots, 2 * ny, m // 4, width), jnp.float32),
            pltpu.VMEM((m // 2, width), jnp.bfloat16),
            pltpu.SemaphoreType.DMA((2,)),
            pltpu.SemaphoreType.DMA((2, total)),
            pltpu.SemaphoreType.DMA((total,)),
            pltpu.SemaphoreType.DMA((slots,)),
            pltpu.SemaphoreType.DMA((slots,)),
            pltpu.SemaphoreType.DMA((slots, 2)),
            pltpu.SemaphoreType.DMA((slots, 2 * ny)),
            pltpu.SemaphoreType.DMA((1,)),
            pltpu.SemaphoreType.DMA((own_rows // m,)),
            pltpu.SemaphoreType.REGULAR((ny + 1,)),
        ],
        compiler_params=pltpu.CompilerParams(
            collective_id=0, has_side_effects=True, vmem_limit_bytes=62 * 2**20
        ),
        cost_estimate=pl.CostEstimate(
            flops=2 * tokens * width * hidden,
            bytes_accessed=2 * width * hidden,
            transcendentals=0,
        ),
        name="input_gradient",
    )(cotangent, weight, up3, down3)


def on_device(n, rows, inputs, cotangent, weight, adapter_down_factor, adapter_up_factor):
    row_position = lax.axis_index("row")
    column_position = lax.axis_index("col")
    width_row_block = inputs.shape[1]
    width_columns = weight.shape[0]
    hidden_columns = cotangent.shape[1]
    down_factor_rows = lax.dynamic_slice_in_dim(
        adapter_down_factor, row_position * width_row_block, width_row_block, 0
    )
    down_factor_columns = lax.dynamic_slice_in_dim(
        adapter_down_factor, column_position * width_columns, width_columns, 0
    )
    up_weight_slice = lax.dynamic_slice_in_dim(
        adapter_up_factor, row_position * hidden_columns, hidden_columns, 1
    )
    grad_input = input_gradient(
        n, rows, cotangent, weight, up_weight_slice, down_factor_columns
    )
    low_part = contract_trailing_axis(cotangent, up_weight_slice)
    proj_part = jnp.dot(inputs, down_factor_rows, preferred_element_type=jnp.float32)
    gradient_lowrank, projected_rows = lax.psum((low_part, proj_part), "row")
    part_a = scaling * jnp.dot(
        inputs.astype(jnp.float32).T, gradient_lowrank, precision=lax.Precision.HIGHEST
    )
    part_b = scaling * jnp.dot(
        projected_rows.T, cotangent.astype(jnp.float32), precision=lax.Precision.HIGHEST
    )
    grad_a, grad_b = lax.psum((part_a, part_b), "col")
    return (grad_input, grad_a, grad_b)


def solution(mesh):
    in_specs = (P("col", "row"), P("col", "row"), P("col", "row"), P(), P())
    out_specs = (P("row", "col"), P("row", None), P(None, "row"))
    body = functools.partial(on_device, mesh.shape["col"], mesh.shape["row"])
    return jax.shard_map(
        body, mesh=mesh, in_specs=in_specs, out_specs=out_specs, check_vma=False
    )
```
